32 devices in a mesh: groups: 2 (over x), tensor: 8 (over z, y), examples: 2 (over core).
Axes of the slice: x: 2, y: 2, z: 4, core: 2. Of those that a mesh axis runs over, the one named last changes fastest.
Arguments:
- act_up: bfloat16 [64, 16, 8192], P(('groups', 'examples'), None, 'tensor'), parts along dimension 0, may hold values from -6 to 6
- grad_up: bfloat16 [64, 16, 28672], P(('groups', 'examples'), None, 'tensor'), parts along dimension 0, may hold values from -6 to 6
- act_down: bfloat16 [64, 16, 28672], P(('groups', 'examples'), None, 'tensor'), parts along dimension 0, may hold values from -6 to 6
- grad_down: bfloat16 [64, 16, 8192], P(('groups', 'examples'), None, 'tensor'), parts along dimension 0, may hold values from -6 to 6
- basis_act_up: bfloat16 [8192, 64], P('tensor'), may hold values from -0.0625 to 0.0625
- basis_grad_up: bfloat16 [28672, 128], P('tensor'), may hold values from -0.03125 to 0.03125
- basis_act_down: bfloat16 [28672, 64], P('tensor'), may hold values from -0.03125 to 0.03125
- basis_grad_down: bfloat16 [8192, 128], P('tensor'), may hold values from -0.0625 to 0.0625
Outputs:
- feature_up: float32 [4, 16, 8192], P(('groups', 'examples'), 'tensor'), parts along dimension 0
- gram_up: float32 [16384, 8192], P(('groups', 'examples'), 'tensor'), parts along dimension 0
- feature_down: float32 [4, 16, 8192], P(('groups', 'examples'), 'tensor'), parts along dimension 0
- gram_down: float32 [16384, 8192], P(('groups', 'examples'), 'tensor'), parts along dimension 0
The draws below stay inside these ranges and needn't reach their ends.
There are 2 independent parts, one for each index of `groups`. The reference program is written for one: setup_inputs(seed, part) draws one part's arguments, and reference() takes and returns one part's arrays. A program takes and returns all parts, laid end to end along the dimension named above; an argument that names none is the same for every part. Nothing has to cross between parts.
All inputs are finite; a program needn't handle non-finite values.
Results may differ from the reference program's by a relative error of at most 0.0003.
Values sent between devices are 32-bit elements; how exact they have to be, the bound alone decides.
A program may use at most 128 MiB of HBM per device.

```python
import math
import jax
import jax.numpy as jnp
from jax import lax

D = 8192
FF = 28672
RIN = 64
ROUT = 128
SEQ = 16
FEAT = 8192
E_DEV = 16
EXAMPLES = 32
N_EXAMPLES = 2


def level_of(stream_key, dims, split, low, largest):
    def one(position, blocks):
        heights = jax.random.uniform(jax.random.fold_in(jax.random.fold_in(stream_key, 6), position), (blocks,), jnp.float32, low / len(split), largest / len(split))
        return jnp.repeat(jnp.exp(heights), dims[position] // blocks).reshape((-1,) + (1,) * (len(dims) - position - 1))

    loudness = one(*split[0])
    for cut in split[1:]:
        loudness = loudness * one(*cut)
    return loudness


def noise(own_key, extent, width, limit, cuts=(), kind=jnp.bfloat16):
    level = level_of(own_key, extent, cuts, -0.22, 0.18) if cuts else 1.0
    array = jax.random.normal(own_key, extent, jnp.float32) * width * level
    return jnp.minimum(jnp.maximum(array, -limit), limit).astype(kind)


def setup_inputs(seed: int = 0, part: int = 0) -> dict:
    streams_of = jax.random.split(jax.random.key(seed), 9)
    part_keys = jax.random.split(jax.random.fold_in(streams_of[8], part), 9)
    return {
        "act_up": noise(part_keys[0], (EXAMPLES, SEQ, D), 1.0, 6.0, ((0, 2), (2, 8))),
        "grad_up": noise(part_keys[1], (EXAMPLES, SEQ, FF), 1.0, 6.0, ((0, 2), (2, 8))),
        "act_down": noise(part_keys[2], (EXAMPLES, SEQ, FF), 1.0, 6.0, ((0, 2), (2, 8))),
        "grad_down": noise(part_keys[3], (EXAMPLES, SEQ, D), 1.0, 6.0, ((0, 2), (2, 8))),
        "basis_act_up": noise(streams_of[4], (D, RIN), D ** -0.5, 0.0625, ((0, 8),)),
        "basis_grad_up": noise(streams_of[5], (FF, ROUT), FF ** -0.5, 0.03125, ((0, 8),)),
        "basis_act_down": noise(streams_of[6], (FF, RIN), FF ** -0.5, 0.03125, ((0, 8),)),
        "basis_grad_down": noise(streams_of[7], (D, ROUT), D ** -0.5, 0.0625, ((0, 8),)),
    }


def project(acts, basis):
    flat = acts.reshape(acts.shape[0] * acts.shape[1], acts.shape[2])
    product = jnp.dot(flat, basis, preferred_element_type=jnp.float32)
    return product.reshape(acts.shape[0], acts.shape[1], basis.shape[1])

def features(proj_act, proj_grad):
    summed = jnp.einsum('bsa,bsc->bac', proj_grad, proj_act, precision=lax.Precision.HIGHEST)
    summed = summed / math.sqrt(SEQ)
    return summed.reshape(summed.shape[0], summed.shape[1] * summed.shape[2])

def gram_of(feats):
    return jnp.dot(feats.T, feats, precision=lax.Precision.HIGHEST) / EXAMPLES

def reference(act_up, grad_up, act_down, grad_down, basis_act_up, basis_grad_up, basis_act_down, basis_grad_down):
    feat_one = features(project(act_up, basis_act_up), project(grad_up, basis_grad_up))
    feat_two = features(project(act_down, basis_act_down), project(grad_down, basis_grad_down))
    gram_one = gram_of(feat_one)
    gram_two = gram_of(feat_two)
    return (feat_one.reshape(N_EXAMPLES, E_DEV, FEAT), gram_one, feat_two.reshape(N_EXAMPLES, E_DEV, FEAT), gram_two)
```

```python
import functools
import math

import jax
import jax.numpy as jnp
from jax import lax
from jax.experimental import pallas as pl
from jax.experimental.pallas import tpu as pltpu
from jax.sharding import PartitionSpec as P

LANES = 128
MESH = pl.DeviceIdType.MESH
VMEM_LIMIT = 56 * 1024 * 1024


def exchange_kernel(n_tensor, n_core, own_rows, act_up, grad_up, act_down, grad_down, b_au, b_gu, b_ad, b_gd,
                    gathered, v_au, v_gu, v_ad, v_gd, w_au, w_gu, w_ad, w_gd,
                    part, pair_in, line_in, whole, load_sem, out_sem,
                    pair_send, pair_recv, line_send, line_recv, gat_send, gat_recv,
                    back_send, back_recv, core_send, core_recv):
    n_line = n_tensor // 2
    t = lax.axis_index("tensor")
    e = lax.axis_index("examples")
    z, y = t // 2, t % 2
    pair = {"tensor": z * 2 + 1 - y}

    def line(step):
        return {"tensor": lax.rem(z + step, n_line) * 2 + y}

    sources = ((grad_down, b_gd, v_gd, w_gd), (grad_up, b_gu, v_gu, w_gu),
               (act_up, b_au, v_au, w_au), (act_down, b_ad, v_ad, w_ad))
    loads = []
    for i, (act, basis, v, w) in enumerate(sources):
        one = pltpu.make_async_copy(act, v, load_sem.at[2 * i])
        two = pltpu.make_async_copy(basis, w, load_sem.at[2 * i + 1])
        one.start()
        two.start()
        loads.append((one, two))

    barrier = pltpu.get_barrier_semaphore()
    pl.semaphore_signal(barrier, inc=1, device_id=pair, device_id_type=MESH)
    for step in range(1, n_line):
        pl.semaphore_signal(barrier, inc=1, device_id=line(step), device_id_type=MESH)
    for step in range(1, n_core):
        pl.semaphore_signal(barrier, inc=1, device_id={"examples": lax.rem(e + step, n_core)}, device_id_type=MESH)

    def product(i):
        loads[i][0].wait()
        loads[i][1].wait()
        v, w = sources[i][2:]
        return jnp.dot(v[...], w[...], preferred_element_type=jnp.float32)

    pair_copies = []
    for c in range(3):
        value = product(c) if c < 2 else jnp.concatenate([product(2), product(3)], axis=1)
        for owner in range(n_tensor):
            part[c, owner % 2, owner // 2] = value[owner * own_rows:(owner + 1) * own_rows]
        if c == 0:
            pl.semaphore_wait(barrier, 1 + (n_line - 1) + (n_core - 1))
        copy = pltpu.make_async_remote_copy(
            src_ref=part.at[c, 1 - y], dst_ref=pair_in.at[c], send_sem=pair_send.at[c], recv_sem=pair_recv.at[c],
            device_id=pair, device_id_type=MESH)
        copy.start()
        pair_copies.append(copy)

    line_copies = []
    for c in range(3):
        pair_copies[c].wait_recv()
        pair_in[c] = pair_in[c] + part[c, y]
        copies = []
        for step in range(1, n_line):
            copy = pltpu.make_async_remote_copy(
                src_ref=pair_in.at[c, lax.rem(z + step, n_line)], dst_ref=line_in.at[c, step - 1],
                send_sem=line_send.at[c, step - 1], recv_sem=line_recv.at[c, step - 1],
                device_id=line(step), device_id_type=MESH)
            copy.start()
            copies.append(copy)
        line_copies.append(copies)

    gat_copies = []
    for c in range(3):
        total = pair_in[c, z]
        for step in range(1, n_line):
            line_copies[c][step - 1].wait_recv()
            total = total + line_in[c, step - 1]
        whole[c, e, y, z] = total
        copies = []
        for step in range(1, n_line):
            copy = pltpu.make_async_remote_copy(
                src_ref=whole.at[c, e, y, z], dst_ref=whole.at[c, e, y, z],
                send_sem=gat_send.at[c, step - 1], recv_sem=gat_recv.at[c, step - 1],
                device_id=line(step), device_id_type=MESH)
            copy.start()
            copies.append(copy)
        gat_copies.append(copies)

    back_copies, core_copies, outs = [], [], []

    def to_cores(c, side, half):
        for step in range(1, n_core):
            copy = pltpu.make_async_remote_copy(
                src_ref=whole.at[c, e, half], dst_ref=whole.at[c, e, half],
                send_sem=core_send.at[c, side, step - 1], recv_sem=core_recv.at[c, side, step - 1],
                device_id={"examples": lax.rem(e + step, n_core)}, device_id_type=MESH)
            copy.start()
            core_copies.append(copy)

    for c in range(3):
        for copy in gat_copies[c]:
            copy.wait_recv()
        copy = pltpu.make_async_remote_copy(
            src_ref=whole.at[c, e, y], dst_ref=whole.at[c, e, y], send_sem=back_send.at[c], recv_sem=back_recv.at[c],
            device_id=pair, device_id_type=MESH)
        copy.start()
        back_copies.append(copy)
        to_cores(c, 0, y)
    for c in range(3):
        back_copies[c].wait_recv()
        to_cores(c, 1, 1 - y)
    for copy in core_copies:
        copy.wait_recv()
    out = pltpu.make_async_copy(whole, gathered, out_sem)
    out.start()
    out.wait()
    for copies in [pair_copies, back_copies, core_copies] + line_copies + gat_copies:
        for copy in copies:
            copy.wait_send()


def split_lanes(value):
    high = value.astype(jnp.bfloat16)
    low = (value - high.astype(jnp.float32)).astype(jnp.bfloat16)
    return high, low


def features_of(grad_pair, act_tile, first, columns, seq_len, width_in):
    width_out = grad_pair.shape[1] // 2
    batch = grad_pair.shape[0] // seq_len
    pick = lax.broadcasted_iota(jnp.int32, (width_out, columns), 0) - lax.broadcasted_iota(
        jnp.int32, (width_out, columns), 1) // width_in
    pick = jnp.where(pick == first, 1.0, 0.0).astype(jnp.bfloat16)
    pick = jnp.concatenate([pick, pick], axis=0)
    spread = jnp.dot(grad_pair, pick, preferred_element_type=jnp.float32)
    pieces = []
    for start in range(0, columns, LANES):
        piece = spread[:, start:start + LANES] * act_tile
        pieces.append(piece.reshape(seq_len, batch, LANES).sum(axis=0))
    return jnp.concatenate(pieces, axis=1)


def gram_kernel(n_tensor, n_core, seq_len, width_in, block, slots,
                gathered, feat_up, gram_up, feat_down, gram_down,
                rows, grad_pair, act_tile, own_grad, own_act, right, own_feat, held, load_sem, feat_sem, gram_sem):
    t = lax.axis_index("tensor")
    e = lax.axis_index("examples")
    n_line = n_tensor // 2
    batch = gathered.shape[1] // seq_len
    width_out = gathered.shape[2]
    own = own_grad.shape[0] // seq_len
    total_examples = batch
    a_rows = width_out // n_core
    a_cols = width_out // n_tensor
    a_block = block // width_in
    n_blocks = a_rows // a_block
    feat_part = own_feat.shape[2] // n_blocks
    a_part = feat_part // width_in
    own_at = pl.multiple_of((e * n_tensor + (t % 2) * n_line + t // 2) * (own * seq_len), own * seq_len)
    scale = 1.0 / math.sqrt(seq_len)

    load = pltpu.make_async_copy(gathered, rows, load_sem)
    load.start()
    load.wait()

    for layer, (gram, feat) in enumerate(((gram_up, feat_up), (gram_down, feat_down))):
        chunk = 1 - layer
        lane = lax.broadcasted_iota(jnp.int32, (batch, LANES), 1)
        for s in range(seq_len):
            at = pl.ds(s * batch, batch)
            high, low = split_lanes(rows[chunk, pl.ds(s, batch, seq_len), :])
            grad_pair[at, :width_out] = high
            grad_pair[at, width_out:] = low
            act = rows[2, pl.ds(s, batch, seq_len), :] * scale
            turned = pltpu.roll(act, width_in, axis=1)
            first, second = (act, turned) if layer == 0 else (turned, act)
            act_tile[at, :] = jnp.where(lane < width_in, first, second)
        lane = lax.broadcasted_iota(jnp.int32, (own, LANES), 1)
        grads, acts = [], []
        for s in range(seq_len):
            grads.append(rows[chunk, pl.ds(own_at + s, own, seq_len), :])
            act = rows[2, pl.ds(own_at + s, own, seq_len), :] * scale
            turned = pltpu.roll(act, width_in, axis=1)
            first, second = (act, turned) if layer == 0 else (turned, act)
            acts.append(jnp.where(lane < width_in, first, second))
        high, low = split_lanes(jnp.concatenate(grads, axis=0))
        own_grad[:, :width_out] = high
        own_grad[:, width_out:] = low
        own_act[...] = jnp.concatenate(acts, axis=0)

        columns = a_cols * width_in
        value = features_of(grad_pair[...], act_tile[...], t * a_cols, columns, seq_len, width_in)
        high, low = split_lanes(value * (1.0 / total_examples))
        right[0:batch] = high
        right[batch:2 * batch] = low
        right[2 * batch:] = high

        def step(i, carry):
            slot = lax.rem(i + layer * n_blocks, slots)
            value = features_of(grad_pair[...], act_tile[...], e * a_rows + i * a_block, block, seq_len, width_in)
            high, low = split_lanes(value)
            left = jnp.concatenate([high, high, low], axis=0)
            product = lax.dot_general(left, right[...], (((0,), (0,)), ((), ())), preferred_element_type=jnp.float32)

            def wait():
                pltpu.make_async_copy(held.at[slot], gram.at[pl.ds(0, block)], gram_sem.at[slot]).wait()

            if layer == 0:
                pl.when(i >= slots)(wait)
            else:
                wait()
            held[slot] = product
            pltpu.make_async_copy(
                held.at[slot], gram.at[pl.ds(pl.multiple_of(i * block, block), block)], gram_sem.at[slot]).start()
            value = features_of(own_grad[...], own_act[...], i * a_part, feat_part, seq_len, width_in)
            own_feat[layer, :, pl.ds(pl.multiple_of(i * feat_part, feat_part), feat_part)] = value
            return carry

        lax.fori_loop(0, n_blocks, step, 0)
        pltpu.make_async_copy(own_feat.at[layer], feat, feat_sem.at[layer]).start()

    for slot in range(slots):
        pltpu.make_async_copy(held.at[slot], gram_down.at[pl.ds(0, block)], gram_sem.at[slot]).wait()
    for layer, feat in enumerate((feat_up, feat_down)):
        pltpu.make_async_copy(own_feat.at[layer], feat, feat_sem.at[layer]).wait()


def shards(n_tensor, n_core, act_up, grad_up, act_down, grad_down, b_au, b_gu, b_ad, b_gd):
    ex_local, seq_len = act_up.shape[0], act_up.shape[1]
    token_rows = ex_local * seq_len
    acts = [a.reshape(token_rows, a.shape[2]) for a in (act_up, grad_up, act_down, grad_down)]
    bases = [b_au, b_gu, b_ad, b_gd]
    width_in, width_out = b_au.shape[1], b_gu.shape[1]
    own_rows = token_rows // n_tensor
    owned = own_rows // seq_len
    n_line = n_tensor // 2
    f32 = jnp.float32
    any_space = pl.BlockSpec(memory_space=pl.ANY)
    dma = pltpu.SemaphoreType.DMA
    steps = max(n_line - 1, 1)
    gathered = pl.pallas_call(
        functools.partial(exchange_kernel, n_tensor, n_core, own_rows),
        out_shape=jax.ShapeDtypeStruct((3, n_core, 2, n_line, own_rows, LANES), f32),
        in_specs=[any_space] * 8,
        out_specs=any_space,
        scratch_shapes=[pltpu.VMEM(a.shape, a.dtype) for a in acts + bases] + [
            pltpu.VMEM((3, 2, n_line, own_rows, LANES), f32),
            pltpu.VMEM((3, n_line, own_rows, LANES), f32),
            pltpu.VMEM((3, steps, own_rows, LANES), f32),
            pltpu.VMEM((3, n_core, 2, n_line, own_rows, LANES), f32),
            dma((8,)), dma,
            dma((3,)), dma((3,)), dma((3, steps)), dma((3, steps)), dma((3, steps)), dma((3, steps)),
            dma((3,)), dma((3,)), dma((3, 2, n_core - 1)), dma((3, 2, n_core - 1)),
        ],
        compiler_params=pltpu.CompilerParams(
            collective_id=0, has_side_effects=True, vmem_limit_bytes=VMEM_LIMIT),
        name="project_and_gather",
    )(*acts, *bases)

    tokens = n_core * token_rows
    batch = tokens // seq_len
    feat = width_in * width_out
    row_width, col_width = feat // n_core, feat // n_tensor
    block, slots = 512, 4
    shape = jax.ShapeDtypeStruct
    bf16 = jnp.bfloat16
    feature_one, gram_one, feature_two, gram_two = pl.pallas_call(
        functools.partial(gram_kernel, n_tensor, n_core, seq_len, width_in, block, slots),
        out_shape=[shape((owned, feat), f32), shape((row_width, col_width), f32)] * 2,
        in_specs=[any_space],
        out_specs=[any_space] * 4,
        scratch_shapes=[
            pltpu.VMEM((3, tokens, LANES), f32),
            pltpu.VMEM((tokens, 2 * width_out), bf16),
            pltpu.VMEM((tokens, LANES), f32),
            pltpu.VMEM((own_rows, 2 * width_out), bf16),
            pltpu.VMEM((own_rows, LANES), f32),
            pltpu.VMEM((3 * batch, col_width), bf16),
            pltpu.VMEM((2, owned, feat), f32),
            pltpu.VMEM((slots, block, col_width), f32),
            dma, dma((2,)), dma((slots,)),
        ],
        compiler_params=pltpu.CompilerParams(vmem_limit_bytes=VMEM_LIMIT),
        name="features_and_gram",
    )(gathered.reshape(3, tokens, LANES))
    return (
        feature_one.reshape(1, owned, feat),
        gram_one,
        feature_two.reshape(1, owned, feat),
        gram_two,
    )


def solution(mesh):
    in_specs = (
        P(("groups", "examples"), None, "tensor"),
        P(("groups", "examples"), None, "tensor"),
        P(("groups", "examples"), None, "tensor"),
        P(("groups", "examples"), None, "tensor"),
        P("tensor", None),
        P("tensor", None),
        P("tensor", None),
        P("tensor", None),
    )
    out_specs = (
        P(("groups", "examples"), "tensor", None),
        P(("groups", "examples"), "tensor"),
        P(("groups", "examples"), "tensor", None),
        P(("groups", "examples"), "tensor"),
    )
    body = functools.partial(shards, mesh.shape["tensor"], mesh.shape["examples"])
    return jax.shard_map(body, mesh=mesh, in_specs=in_specs, out_specs=out_specs, check_vma=False)
```

```python
import functools
import math

import jax
import jax.numpy as jnp
from jax import lax
from jax.experimental import pallas as pl
from jax.experimental.pallas import tpu as pltpu
from jax.sharding import PartitionSpec as P

LANES = 128
TILE = 256
MESH = pl.DeviceIdType.MESH
VMEM_LIMIT = 56 * 1024 * 1024


def exchange_kernel(n_tensor, n_core, own_rows, act_up, grad_up, act_down, grad_down, b_au, b_gu, b_ad, b_gd,
                    gathered, v_au, v_gu, v_ad, v_gd, w_au, w_gu, w_ad, w_gd,
                    part, pair_in, line_in, whole, load_sem, out_sem,
                    pair_send, pair_recv, line_send, line_recv, gat_send, gat_recv,
                    back_send, back_recv, core_send, core_recv):
    n_line = n_tensor // 2
    t = lax.axis_index("tensor")
    e = lax.axis_index("examples")
    z, y = t // 2, t % 2
    pair = {"tensor": z * 2 + 1 - y}

    def line(step):
        return {"tensor": lax.rem(z + step, n_line) * 2 + y}

    sources = ((grad_down, b_gd, v_gd, w_gd), (grad_up, b_gu, v_gu, w_gu),
               (act_up, b_au, v_au, w_au), (act_down, b_ad, v_ad, w_ad))
    loads = []
    for i, (act, basis, v, w) in enumerate(sources):
        one = pltpu.make_async_copy(act, v, load_sem.at[2 * i])
        two = pltpu.make_async_copy(basis, w, load_sem.at[2 * i + 1])
        one.start()
        two.start()
        loads.append((one, two))

    barrier = pltpu.get_barrier_semaphore()
    pl.semaphore_signal(barrier, inc=1, device_id=pair, device_id_type=MESH)
    for step in range(1, n_line):
        pl.semaphore_signal(barrier, inc=1, device_id=line(step), device_id_type=MESH)
    for step in range(1, n_core):
        pl.semaphore_signal(barrier, inc=1, device_id={"examples": lax.rem(e + step, n_core)}, device_id_type=MESH)

    def product(i):
        loads[i][0].wait()
        loads[i][1].wait()
        v, w = sources[i][2:]
        dims = (((1,), (0 if i < 2 else 1,)), ((), ()))
        return lax.dot_general(v[...], w[...], dims, preferred_element_type=jnp.float32)

    pair_copies = []
    for c in range(3):
        value = product(c) if c < 2 else jnp.concatenate([product(2), product(3)], axis=1)
        for owner in range(n_tensor):
            part[c, owner % 2, owner // 2] = value[owner * own_rows:(owner + 1) * own_rows]
        if c == 0:
            pl.semaphore_wait(barrier, 1 + (n_line - 1) + (n_core - 1))
        copy = pltpu.make_async_remote_copy(
            src_ref=part.at[c, 1 - y], dst_ref=pair_in.at[c], send_sem=pair_send.at[c], recv_sem=pair_recv.at[c],
            device_id=pair, device_id_type=MESH)
        copy.start()
        pair_copies.append(copy)

    line_copies = []
    for c in range(3):
        pair_copies[c].wait_recv()
        pair_in[c] = pair_in[c] + part[c, y]
        copies = []
        for step in range(1, n_line):
            copy = pltpu.make_async_remote_copy(
                src_ref=pair_in.at[c, lax.rem(z + step, n_line)], dst_ref=line_in.at[c, step - 1],
                send_sem=line_send.at[c, step - 1], recv_sem=line_recv.at[c, step - 1],
                device_id=line(step), device_id_type=MESH)
            copy.start()
            copies.append(copy)
        line_copies.append(copies)

    gat_copies = []
    for c in range(3):
        total = pair_in[c, z]
        for step in range(1, n_line):
            line_copies[c][step - 1].wait_recv()
            total = total + line_in[c, step - 1]
        whole[c, e, y, z] = total
        copies = []
        for step in range(1, n_line):
            copy = pltpu.make_async_remote_copy(
                src_ref=whole.at[c, e, y, z], dst_ref=whole.at[c, e, y, z],
                send_sem=gat_send.at[c, step - 1], recv_sem=gat_recv.at[c, step - 1],
                device_id=line(step), device_id_type=MESH)
            copy.start()
            copies.append(copy)
        gat_copies.append(copies)

    back_copies, core_copies, outs = [], [], []

    def to_cores(c, side, half):
        for step in range(1, n_core):
            copy = pltpu.make_async_remote_copy(
                src_ref=whole.at[c, e, half], dst_ref=whole.at[c, e, half],
                send_sem=core_send.at[c, side, step - 1], recv_sem=core_recv.at[c, side, step - 1],
                device_id={"examples": lax.rem(e + step, n_core)}, device_id_type=MESH)
            copy.start()
            core_copies.append(copy)

    for c in range(3):
        for copy in gat_copies[c]:
            copy.wait_recv()
        copy = pltpu.make_async_remote_copy(
            src_ref=whole.at[c, e, y], dst_ref=whole.at[c, e, y], send_sem=back_send.at[c], recv_sem=back_recv.at[c],
            device_id=pair, device_id_type=MESH)
        copy.start()
        back_copies.append(copy)
        to_cores(c, 0, y)
    for c in range(3):
        back_copies[c].wait_recv()
        to_cores(c, 1, 1 - y)
    for copy in core_copies:
        copy.wait_recv()
    out = pltpu.make_async_copy(whole, gathered, out_sem)
    out.start()
    out.wait()
    for copies in [pair_copies, back_copies, core_copies] + line_copies + gat_copies:
        for copy in copies:
            copy.wait_send()


def split_lanes(value):
    high = value.astype(jnp.bfloat16)
    low = (value - high.astype(jnp.float32)).astype(jnp.bfloat16)
    return high, low


def features_of(grad_pair, act_tile, first, columns, seq_len, width_in):
    width_out = grad_pair.shape[1] // 2
    batch = grad_pair.shape[0] // seq_len
    tile = min(TILE, columns)
    pieces = []
    for start in range(0, columns, tile):
        pick = lax.broadcasted_iota(jnp.int32, (width_out, tile), 0) - (
            lax.broadcasted_iota(jnp.int32, (width_out, tile), 1) + start) // width_in
        pick = jnp.where(pick == first, 1.0, 0.0).astype(jnp.bfloat16)
        pick = jnp.concatenate([pick, pick], axis=0)
        spread = jnp.dot(grad_pair[...], pick, preferred_element_type=jnp.float32)
        for part in range(0, tile, LANES):
            piece = spread[:, part:part + LANES] * act_tile[...]
            pieces.append(piece.reshape(seq_len, batch, LANES).sum(axis=0))
    return jnp.concatenate(pieces, axis=1)


def gram_kernel(n_tensor, n_core, seq_len, width_in, block, slots,
                gathered, feat_up, gram_up, feat_down, gram_down,
                rows, grad_pair, act_tile, own_grad, own_act, right, own_feat, held, load_sem, feat_sem, gram_sem):
    t = lax.axis_index("tensor")
    e = lax.axis_index("examples")
    n_line = n_tensor // 2
    batch = gathered.shape[1] // seq_len
    width_out = gathered.shape[2]
    own = own_grad.shape[0] // seq_len
    total_examples = batch
    a_rows = width_out // n_core
    a_cols = width_out // n_tensor
    a_block = block // width_in
    n_blocks = a_rows // a_block
    feat_part = own_feat.shape[2] // n_blocks
    a_part = feat_part // width_in
    own_at = pl.multiple_of((e * n_tensor + (t % 2) * n_line + t // 2) * (own * seq_len), own * seq_len)
    scale = 1.0 / math.sqrt(seq_len)

    load = pltpu.make_async_copy(gathered, rows, load_sem)
    load.start()
    load.wait()

    for layer, (gram, feat) in enumerate(((gram_up, feat_up), (gram_down, feat_down))):
        chunk = 1 - layer
        lane = lax.broadcasted_iota(jnp.int32, (batch, LANES), 1)
        for s in range(seq_len):
            at = pl.ds(s * batch, batch)
            high, low = split_lanes(rows[chunk, pl.ds(s, batch, seq_len), :])
            grad_pair[at, :width_out] = high
            grad_pair[at, width_out:] = low
            act = rows[2, pl.ds(s, batch, seq_len), :] * scale
            turned = pltpu.roll(act, width_in, axis=1)
            first, second = (act, turned) if layer == 0 else (turned, act)
            act_tile[at, :] = jnp.where(lane < width_in, first, second)
        lane = lax.broadcasted_iota(jnp.int32, (own, LANES), 1)
        grads, acts = [], []
        for s in range(seq_len):
            grads.append(rows[chunk, pl.ds(own_at + s, own, seq_len), :])
            act = rows[2, pl.ds(own_at + s, own, seq_len), :] * scale
            turned = pltpu.roll(act, width_in, axis=1)
            first, second = (act, turned) if layer == 0 else (turned, act)
            acts.append(jnp.where(lane < width_in, first, second))
        high, low = split_lanes(jnp.concatenate(grads, axis=0))
        own_grad[:, :width_out] = high
        own_grad[:, width_out:] = low
        own_act[...] = jnp.concatenate(acts, axis=0)

        columns = a_cols * width_in
        value = features_of(grad_pair, act_tile, t * a_cols, columns, seq_len, width_in)
        high, low = split_lanes(value * (1.0 / total_examples))
        right[0:batch] = high
        right[batch:2 * batch] = low
        right[2 * batch:] = high

        def step(i, carry):
            slot = lax.rem(i + layer * n_blocks, slots)

            def wait():
                pltpu.make_async_copy(held.at[slot], gram.at[pl.ds(0, block)], gram_sem.at[slot]).wait()

            if layer == 0:
                pl.when(i >= slots)(wait)
            else:
                wait()
            value = features_of(grad_pair, act_tile, e * a_rows + i * a_block, block, seq_len, width_in)
            high, low = split_lanes(value)
            left = jnp.concatenate([high, high, low], axis=0)
            for start in range(0, columns, TILE):
                held[slot, :, start:start + TILE] = lax.dot_general(
                    left, right[:, start:start + TILE], (((0,), (0,)), ((), ())),
                    preferred_element_type=jnp.float32)
            pltpu.make_async_copy(
                held.at[slot], gram.at[pl.ds(pl.multiple_of(i * block, block), block)], gram_sem.at[slot]).start()
            value = features_of(own_grad, own_act, i * a_part, feat_part, seq_len, width_in)
            own_feat[layer, :, pl.ds(pl.multiple_of(i * feat_part, feat_part), feat_part)] = value
            return carry

        lax.fori_loop(0, n_blocks, step, 0)
        pltpu.make_async_copy(own_feat.at[layer], feat, feat_sem.at[layer]).start()

    for slot in range(slots):
        pltpu.make_async_copy(held.at[slot], gram_down.at[pl.ds(0, block)], gram_sem.at[slot]).wait()
    for layer, feat in enumerate((feat_up, feat_down)):
        pltpu.make_async_copy(own_feat.at[layer], feat, feat_sem.at[layer]).wait()


def shards(n_tensor, n_core, act_up, grad_up, act_down, grad_down, b_au, b_gu, b_ad, b_gd):
    ex_local, seq_len = act_up.shape[0], act_up.shape[1]
    token_rows = ex_local * seq_len
    acts = [a.reshape(token_rows, a.shape[2]) for a in (act_up, grad_up, act_down, grad_down)]
    bases = [b_au.T, b_gu, b_ad.T, b_gd]
    width_in, width_out = b_au.shape[1], b_gu.shape[1]
    own_rows = token_rows // n_tensor
    owned = own_rows // seq_len
    n_line = n_tensor // 2
    f32 = jnp.float32
    any_space = pl.BlockSpec(memory_space=pl.ANY)
    dma = pltpu.SemaphoreType.DMA
    steps = max(n_line - 1, 1)
    gathered = pl.pallas_call(
        functools.partial(exchange_kernel, n_tensor, n_core, own_rows),
        out_shape=jax.ShapeDtypeStruct((3, n_core, 2, n_line, own_rows, LANES), f32),
        in_specs=[any_space] * 8,
        out_specs=any_space,
        scratch_shapes=[pltpu.VMEM(a.shape, a.dtype) for a in acts + bases] + [
            pltpu.VMEM((3, 2, n_line, own_rows, LANES), f32),
            pltpu.VMEM((3, n_line, own_rows, LANES), f32),
            pltpu.VMEM((3, steps, own_rows, LANES), f32),
            pltpu.VMEM((3, n_core, 2, n_line, own_rows, LANES), f32),
            dma((8,)), dma,
            dma((3,)), dma((3,)), dma((3, steps)), dma((3, steps)), dma((3, steps)), dma((3, steps)),
            dma((3,)), dma((3,)), dma((3, 2, n_core - 1)), dma((3, 2, n_core - 1)),
        ],
        compiler_params=pltpu.CompilerParams(
            collective_id=0, has_side_effects=True, vmem_limit_bytes=VMEM_LIMIT),
        name="project_and_gather",
    )(*acts, *bases)

    tokens = n_core * token_rows
    batch = tokens // seq_len
    feat = width_in * width_out
    row_width, col_width = feat // n_core, feat // n_tensor
    block, slots = 512, 4
    shape = jax.ShapeDtypeStruct
    bf16 = jnp.bfloat16
    feature_one, gram_one, feature_two, gram_two = pl.pallas_call(
        functools.partial(gram_kernel, n_tensor, n_core, seq_len, width_in, block, slots),
        out_shape=[shape((owned, feat), f32), shape((row_width, col_width), f32)] * 2,
        in_specs=[any_space],
        out_specs=[any_space] * 4,
        scratch_shapes=[
            pltpu.VMEM((3, tokens, LANES), f32),
            pltpu.VMEM((tokens, 2 * width_out), bf16),
            pltpu.VMEM((tokens, LANES), f32),
            pltpu.VMEM((own_rows, 2 * width_out), bf16),
            pltpu.VMEM((own_rows, LANES), f32),
            pltpu.VMEM((3 * batch, col_width), bf16),
            pltpu.VMEM((2, owned, feat), f32),
            pltpu.VMEM((slots, block, col_width), f32),
            dma, dma((2,)), dma((slots,)),
        ],
        compiler_params=pltpu.CompilerParams(vmem_limit_bytes=VMEM_LIMIT),
        name="features_and_gram",
    )(gathered.reshape(3, tokens, LANES))
    return (
        feature_one.reshape(1, owned, feat),
        gram_one,
        feature_two.reshape(1, owned, feat),
        gram_two,
    )


def solution(mesh):
    in_specs = (
        P(("groups", "examples"), None, "tensor"),
        P(("groups", "examples"), None, "tensor"),
        P(("groups", "examples"), None, "tensor"),
        P(("groups", "examples"), None, "tensor"),
        P("tensor", None),
        P("tensor", None),
        P("tensor", None),
        P("tensor", None),
    )
    out_specs = (
        P(("groups", "examples"), "tensor", None),
        P(("groups", "examples"), "tensor"),
        P(("groups", "examples"), "tensor", None),
        P(("groups", "examples"), "tensor"),
    )
    body = functools.partial(shards, mesh.shape["tensor"], mesh.shape["examples"])
    return jax.shard_map(body, mesh=mesh, in_specs=in_specs, out_specs=out_specs, check_vma=False)
```

```python
import functools
import math

import jax
import jax.numpy as jnp
from jax import lax
from jax.experimental import pallas as pl
from jax.experimental.pallas import tpu as pltpu
from jax.sharding import PartitionSpec as P

LANES = 128
TILE = 256
GROUPS = ((0, 1), (1, 2), (2, 3))
MESH = pl.DeviceIdType.MESH
VMEM_LIMIT = 56 * 1024 * 1024


def exchange_kernel(n_tensor, n_core, own_rows, act_up, grad_up, act_down, grad_down, b_au, b_gu, b_ad, b_gd,
                    gathered, v_au, v_gu, v_ad, v_gd, w_au, w_gu, w_ad, w_gd,
                    part, pair_in, line_in, whole, load_sem, out_sem,
                    pair_send, pair_recv, line_send, line_recv, gat_send, gat_recv,
                    back_send, back_recv, core_send, core_recv):
    n_line = n_tensor // 2
    t = lax.axis_index("tensor")
    e = lax.axis_index("examples")
    z, y = t // 2, t % 2
    pair = {"tensor": z * 2 + 1 - y}

    def line(step):
        return {"tensor": lax.rem(z + step, n_line) * 2 + y}

    sources = ((grad_down, b_gd, v_gd, w_gd), (grad_up, b_gu, v_gu, w_gu),
               (act_up, b_au, v_au, w_au), (act_down, b_ad, v_ad, w_ad))
    loads = []
    for i, (act, basis, v, w) in enumerate(sources):
        one = pltpu.make_async_copy(act, v, load_sem.at[2 * i])
        two = pltpu.make_async_copy(basis, w, load_sem.at[2 * i + 1])
        one.start()
        two.start()
        loads.append((one, two))

    barrier = pltpu.get_barrier_semaphore()
    pl.semaphore_signal(barrier, inc=1, device_id=pair, device_id_type=MESH)
    for step in range(1, n_line):
        pl.semaphore_signal(barrier, inc=1, device_id=line(step), device_id_type=MESH)
    for step in range(1, n_core):
        pl.semaphore_signal(barrier, inc=1, device_id={"examples": lax.rem(e + step, n_core)}, device_id_type=MESH)

    def product(i):
        loads[i][0].wait()
        loads[i][1].wait()
        v, w = sources[i][2:]
        dims = (((1,), (0 if i < 2 else 1,)), ((), ()))
        return lax.dot_general(v[...], w[...], dims, preferred_element_type=jnp.float32)

    pair_copies = []
    for g, (lo, hi) in enumerate(GROUPS):
        for c in range(lo, hi):
            value = product(c) if c < 2 else jnp.concatenate([product(2), product(3)], axis=1)
            for owner in range(n_tensor):
                part[c, owner % 2, owner // 2] = value[owner * own_rows:(owner + 1) * own_rows]
        if g == 0:
            pl.semaphore_wait(barrier, 1 + (n_line - 1) + (n_core - 1))
        copy = pltpu.make_async_remote_copy(
            src_ref=part.at[lo:hi, 1 - y], dst_ref=pair_in.at[lo:hi], send_sem=pair_send.at[g],
            recv_sem=pair_recv.at[g], device_id=pair, device_id_type=MESH)
        copy.start()
        pair_copies.append(copy)

    line_copies = []
    for g, (lo, hi) in enumerate(GROUPS):
        pair_copies[g].wait_recv()
        pair_in[lo:hi] = pair_in[lo:hi] + part[lo:hi, y]
        copies = []
        for step in range(1, n_line):
            copy = pltpu.make_async_remote_copy(
                src_ref=pair_in.at[lo:hi, lax.rem(z + step, n_line)], dst_ref=line_in.at[lo:hi, step - 1],
                send_sem=line_send.at[g, step - 1], recv_sem=line_recv.at[g, step - 1],
                device_id=line(step), device_id_type=MESH)
            copy.start()
            copies.append(copy)
        line_copies.append(copies)

    gat_copies = []
    for g, (lo, hi) in enumerate(GROUPS):
        total = pair_in[lo:hi, z]
        for step in range(1, n_line):
            line_copies[g][step - 1].wait_recv()
            total = total + line_in[lo:hi, step - 1]
        whole[lo:hi, e, y, z] = total
        copies = []
        for step in range(1, n_line):
            copy = pltpu.make_async_remote_copy(
                src_ref=whole.at[lo:hi, e, y, z], dst_ref=whole.at[lo:hi, e, y, z],
                send_sem=gat_send.at[g, step - 1], recv_sem=gat_recv.at[g, step - 1],
                device_id=line(step), device_id_type=MESH)
            copy.start()
            copies.append(copy)
        gat_copies.append(copies)

    back_copies, core_copies = [], []

    def to_cores(g, side, half):
        lo, hi = GROUPS[g]
        for step in range(1, n_core):
            copy = pltpu.make_async_remote_copy(
                src_ref=whole.at[lo:hi, e, half], dst_ref=whole.at[lo:hi, e, half],
                send_sem=core_send.at[g, side, step - 1], recv_sem=core_recv.at[g, side, step - 1],
                device_id={"examples": lax.rem(e + step, n_core)}, device_id_type=MESH)
            copy.start()
            core_copies.append(copy)

    for g, (lo, hi) in enumerate(GROUPS):
        for copy in gat_copies[g]:
            copy.wait_recv()
        copy = pltpu.make_async_remote_copy(
            src_ref=whole.at[lo:hi, e, y], dst_ref=whole.at[lo:hi, e, y], send_sem=back_send.at[g],
            recv_sem=back_recv.at[g], device_id=pair, device_id_type=MESH)
        copy.start()
        back_copies.append(copy)
        to_cores(g, 0, y)
    for g in range(len(GROUPS)):
        back_copies[g].wait_recv()
        to_cores(g, 1, 1 - y)
    for copy in core_copies:
        copy.wait_recv()
    out = pltpu.make_async_copy(whole, gathered, out_sem)
    out.start()
    out.wait()
    for copies in [pair_copies, back_copies, core_copies] + line_copies + gat_copies:
        for copy in copies:
            copy.wait_send()


def split_lanes(value):
    high = value.astype(jnp.bfloat16)
    low = (value - high.astype(jnp.float32)).astype(jnp.bfloat16)
    return high, low


def features_of(grad_pair, act_tile, first, columns, seq_len, width_in):
    width_out = grad_pair.shape[1] // 2
    batch = grad_pair.shape[0] // seq_len
    tile = min(TILE, columns)
    pieces = []
    for start in range(0, columns, tile):
        pick = lax.broadcasted_iota(jnp.int32, (width_out, tile), 0) - (
            lax.broadcasted_iota(jnp.int32, (width_out, tile), 1) + start) // width_in
        pick = jnp.where(pick == first, 1.0, 0.0).astype(jnp.bfloat16)
        pick = jnp.concatenate([pick, pick], axis=0)
        spread = jnp.dot(grad_pair[...], pick, preferred_element_type=jnp.float32)
        for part in range(0, tile, LANES):
            piece = spread[:, part:part + LANES] * act_tile[...]
            pieces.append(piece.reshape(seq_len, batch, LANES).sum(axis=0))
    return jnp.concatenate(pieces, axis=1)


def gram_kernel(n_tensor, n_core, seq_len, width_in, block, slots,
                gathered, feat_up, gram_up, feat_down, gram_down,
                rows, grad_pair, act_tile, own_grad, own_act, right, left_even, left_odd, own_feat, held, load_sem, feat_sem, gram_sem):
    t = lax.axis_index("tensor")
    e = lax.axis_index("examples")
    n_line = n_tensor // 2
    batch = gathered.shape[1] // seq_len
    width_out = gathered.shape[2]
    own = own_grad.shape[0] // seq_len
    total_examples = batch
    a_rows = width_out // n_core
    a_cols = width_out // n_tensor
    a_block = block // width_in
    n_blocks = a_rows // a_block
    feat_part = own_feat.shape[2] // n_blocks
    a_part = feat_part // width_in
    own_at = pl.multiple_of((e * n_tensor + (t % 2) * n_line + t // 2) * (own * seq_len), own * seq_len)
    scale = 1.0 / math.sqrt(seq_len)

    load = pltpu.make_async_copy(gathered, rows, load_sem)
    load.start()
    load.wait()

    for layer, (gram, feat) in enumerate(((gram_up, feat_up), (gram_down, feat_down))):
        chunk = 1 - layer
        lane = lax.broadcasted_iota(jnp.int32, (batch, LANES), 1)
        for s in range(seq_len):
            at = pl.ds(s * batch, batch)
            high, low = split_lanes(rows[chunk, pl.ds(s, batch, seq_len), :])
            grad_pair[at, :width_out] = high
            grad_pair[at, width_out:] = low
            act = rows[2, pl.ds(s, batch, seq_len), :] * scale
            turned = pltpu.roll(act, width_in, axis=1)
            first, second = (act, turned) if layer == 0 else (turned, act)
            act_tile[at, :] = jnp.where(lane < width_in, first, second)
        lane = lax.broadcasted_iota(jnp.int32, (own, LANES), 1)
        grads, acts = [], []
        for s in range(seq_len):
            grads.append(rows[chunk, pl.ds(own_at + s, own, seq_len), :])
            act = rows[2, pl.ds(own_at + s, own, seq_len), :] * scale
            turned = pltpu.roll(act, width_in, axis=1)
            first, second = (act, turned) if layer == 0 else (turned, act)
            acts.append(jnp.where(lane < width_in, first, second))
        high, low = split_lanes(jnp.concatenate(grads, axis=0))
        own_grad[:, :width_out] = high
        own_grad[:, width_out:] = low
        own_act[...] = jnp.concatenate(acts, axis=0)

        columns = a_cols * width_in
        value = features_of(grad_pair, act_tile, t * a_cols, columns, seq_len, width_in)
        high, low = split_lanes(value * (1.0 / total_examples))
        right[0:batch] = high
        right[batch:2 * batch] = low
        right[2 * batch:3 * batch] = high
        if right.shape[0] > 3 * batch:
            right[3 * batch:] = jnp.zeros((right.shape[0] - 3 * batch, columns), jnp.bfloat16)

        def prepare(i, target):
            value = features_of(grad_pair, act_tile, e * a_rows + i * a_block, block, seq_len, width_in)
            high, low = split_lanes(value)
            high, low = high.astype(jnp.float32), low.astype(jnp.float32)
            left = [high, high, low]
            if right.shape[0] > 3 * batch:
                left.append(jnp.zeros((right.shape[0] - 3 * batch, block), jnp.float32))
            target[...] = jnp.concatenate(left, axis=0).T.astype(jnp.bfloat16)

        def step(i, current, following):
            slot = lax.rem(i + layer * n_blocks, slots)

            def wait():
                pltpu.make_async_copy(held.at[slot], gram.at[pl.ds(0, block)], gram_sem.at[slot]).wait()

            if layer == 0:
                pl.when(i >= slots)(wait)
            else:
                wait()
            for start in range(0, columns, TILE):
                held[slot, :, start:start + TILE] = jnp.dot(
                    current[...], right[:, start:start + TILE], preferred_element_type=jnp.float32)
            prepare(lax.rem(i + 1, n_blocks), following)
            value = features_of(own_grad, own_act, i * a_part, feat_part, seq_len, width_in)
            own_feat[layer, :, pl.ds(pl.multiple_of(i * feat_part, feat_part), feat_part)] = value
            pltpu.make_async_copy(
                held.at[slot], gram.at[pl.ds(pl.multiple_of(i * block, block), block)], gram_sem.at[slot]).start()

        def two_steps(i, carry):
            step(2 * i, left_even, left_odd)
            step(2 * i + 1, left_odd, left_even)
            return carry

        prepare(0, left_even)
        lax.fori_loop(0, n_blocks // 2, two_steps, 0)
        pltpu.make_async_copy(own_feat.at[layer], feat, feat_sem.at[layer]).start()

    for slot in range(slots):
        pltpu.make_async_copy(held.at[slot], gram_down.at[pl.ds(0, block)], gram_sem.at[slot]).wait()
    for layer, feat in enumerate((feat_up, feat_down)):
        pltpu.make_async_copy(own_feat.at[layer], feat, feat_sem.at[layer]).wait()


def shards(n_tensor, n_core, act_up, grad_up, act_down, grad_down, b_au, b_gu, b_ad, b_gd):
    ex_local, seq_len = act_up.shape[0], act_up.shape[1]
    token_rows = ex_local * seq_len
    acts = [a.reshape(token_rows, a.shape[2]) for a in (act_up, grad_up, act_down, grad_down)]
    bases = [b_au.T, b_gu, b_ad.T, b_gd]
    width_in, width_out = b_au.shape[1], b_gu.shape[1]
    own_rows = token_rows // n_tensor
    owned = own_rows // seq_len
    n_line = n_tensor // 2
    f32 = jnp.float32
    any_space = pl.BlockSpec(memory_space=pl.ANY)
    dma = pltpu.SemaphoreType.DMA
    steps = max(n_line - 1, 1)
    gathered = pl.pallas_call(
        functools.partial(exchange_kernel, n_tensor, n_core, own_rows),
        out_shape=jax.ShapeDtypeStruct((3, n_core, 2, n_line, own_rows, LANES), f32),
        in_specs=[any_space] * 8,
        out_specs=any_space,
        scratch_shapes=[pltpu.VMEM(a.shape, a.dtype) for a in acts + bases] + [
            pltpu.VMEM((3, 2, n_line, own_rows, LANES), f32),
            pltpu.VMEM((3, n_line, own_rows, LANES), f32),
            pltpu.VMEM((3, steps, own_rows, LANES), f32),
            pltpu.VMEM((3, n_core, 2, n_line, own_rows, LANES), f32),
            dma((8,)), dma,
            dma((3,)), dma((3,)), dma((3, steps)), dma((3, steps)), dma((3, steps)), dma((3, steps)),
            dma((3,)), dma((3,)), dma((3, 2, n_core - 1)), dma((3, 2, n_core - 1)),
        ],
        compiler_params=pltpu.CompilerParams(
            collective_id=0, has_side_effects=True, vmem_limit_bytes=VMEM_LIMIT),
        name="project_and_gather",
    )(*acts, *bases)

    tokens = n_core * token_rows
    batch = tokens // seq_len
    feat = width_in * width_out
    row_width, col_width = feat // n_core, feat // n_tensor
    block, slots = 512, 4
    depth = -(-3 * batch // LANES) * LANES
    shape = jax.ShapeDtypeStruct
    bf16 = jnp.bfloat16
    feature_one, gram_one, feature_two, gram_two = pl.pallas_call(
        functools.partial(gram_kernel, n_tensor, n_core, seq_len, width_in, block, slots),
        out_shape=[shape((owned, feat), f32), shape((row_width, col_width), f32)] * 2,
        in_specs=[any_space],
        out_specs=[any_space] * 4,
        scratch_shapes=[
            pltpu.VMEM((3, tokens, LANES), f32),
            pltpu.VMEM((tokens, 2 * width_out), bf16),
            pltpu.VMEM((tokens, LANES), f32),
            pltpu.VMEM((own_rows, 2 * width_out), bf16),
            pltpu.VMEM((own_rows, LANES), f32),
            pltpu.VMEM((depth, col_width), bf16),
            pltpu.VMEM((block, depth), bf16),
            pltpu.VMEM((block, depth), bf16),
            pltpu.VMEM((2, owned, feat), f32),
            pltpu.VMEM((slots, block, col_width), f32),
            dma, dma((2,)), dma((slots,)),
        ],
        compiler_params=pltpu.CompilerParams(vmem_limit_bytes=VMEM_LIMIT),
        name="features_and_gram",
    )(gathered.reshape(3, tokens, LANES))
    return (
        feature_one.reshape(1, owned, feat),
        gram_one,
        feature_two.reshape(1, owned, feat),
        gram_two,
    )


def solution(mesh):
    in_specs = (
        P(("groups", "examples"), None, "tensor"),
        P(("groups", "examples"), None, "tensor"),
        P(("groups", "examples"), None, "tensor"),
        P(("groups", "examples"), None, "tensor"),
        P("tensor", None),
        P("tensor", None),
        P("tensor", None),
        P("tensor", None),
    )
    out_specs = (
        P(("groups", "examples"), "tensor", None),
        P(("groups", "examples"), "tensor"),
        P(("groups", "examples"), "tensor", None),
        P(("groups", "examples"), "tensor"),
    )
    body = functools.partial(shards, mesh.shape["tensor"], mesh.shape["examples"])
    return jax.shard_map(body, mesh=mesh, in_specs=in_specs, out_specs=out_specs, check_vma=False)
```

```python
import functools
import math

import jax
import jax.numpy as jnp
from jax import lax
from jax.experimental import pallas as pl
from jax.experimental.pallas import tpu as pltpu
from jax.sharding import PartitionSpec as P

LANES = 128
TILE = 256
GROUPS = ((0, 1), (1, 2), (2, 3))
MESH = pl.DeviceIdType.MESH
VMEM_LIMIT = 56 * 1024 * 1024


def exchange_kernel(n_tensor, n_core, own_rows, act_up, grad_up, act_down, grad_down, b_au, b_gu, b_ad, b_gd,
                    gathered, v_au, v_gu, v_ad, v_gd, w_au, w_gu, w_ad, w_gd,
                    part, pair_in, line_in, whole, load_sem, out_sem,
                    pair_send, pair_recv, line_send, line_recv, gat_send, gat_recv,
                    back_send, back_recv, core_send, core_recv):
    n_line = n_tensor // 2
    t = lax.axis_index("tensor")
    e = lax.axis_index("examples")
    z, y = t // 2, t % 2
    pair = {"tensor": z * 2 + 1 - y}

    def line(step):
        return {"tensor": lax.rem(z + step, n_line) * 2 + y}

    sources = ((grad_down, b_gd, v_gd, w_gd), (grad_up, b_gu, v_gu, w_gu),
               (act_up, b_au, v_au, w_au), (act_down, b_ad, v_ad, w_ad))
    loads = []
    for i, (act, basis, v, w) in enumerate(sources):
        one = pltpu.make_async_copy(act, v, load_sem.at[2 * i])
        two = pltpu.make_async_copy(basis, w, load_sem.at[2 * i + 1])
        one.start()
        two.start()
        loads.append((one, two))

    barrier = pltpu.get_barrier_semaphore()
    pl.semaphore_signal(barrier, inc=1, device_id=pair, device_id_type=MESH)
    for step in range(1, n_line):
        pl.semaphore_signal(barrier, inc=1, device_id=line(step), device_id_type=MESH)
    for step in range(1, n_core):
        pl.semaphore_signal(barrier, inc=1, device_id={"examples": lax.rem(e + step, n_core)}, device_id_type=MESH)

    def product(i):
        loads[i][0].wait()
        loads[i][1].wait()
        v, w = sources[i][2:]
        dims = (((1,), (0 if i < 2 else 1,)), ((), ()))
        return lax.dot_general(v[...], w[...], dims, preferred_element_type=jnp.float32)

    pair_copies = []
    for g, (lo, hi) in enumerate(GROUPS):
        for c in range(lo, hi):
            value = product(c) if c < 2 else jnp.concatenate([product(2), product(3)], axis=1)
            for owner in range(n_tensor):
                part[c, owner % 2, owner // 2] = value[owner * own_rows:(owner + 1) * own_rows]
        if g == 0:
            pl.semaphore_wait(barrier, 1 + (n_line - 1) + (n_core - 1))
        copy = pltpu.make_async_remote_copy(
            src_ref=part.at[lo:hi, 1 - y], dst_ref=pair_in.at[lo:hi], send_sem=pair_send.at[g],
            recv_sem=pair_recv.at[g], device_id=pair, device_id_type=MESH)
        copy.start()
        pair_copies.append(copy)

    line_copies = []
    for g, (lo, hi) in enumerate(GROUPS):
        pair_copies[g].wait_recv()
        pair_in[lo:hi] = pair_in[lo:hi] + part[lo:hi, y]
        copies = []
        for step in range(1, n_line):
            copy = pltpu.make_async_remote_copy(
                src_ref=pair_in.at[lo:hi, lax.rem(z + step, n_line)], dst_ref=line_in.at[lo:hi, step - 1],
                send_sem=line_send.at[g, step - 1], recv_sem=line_recv.at[g, step - 1],
                device_id=line(step), device_id_type=MESH)
            copy.start()
            copies.append(copy)
        line_copies.append(copies)

    gat_copies = []
    for g, (lo, hi) in enumerate(GROUPS):
        total = pair_in[lo:hi, z]
        for step in range(1, n_line):
            line_copies[g][step - 1].wait_recv()
            total = total + line_in[lo:hi, step - 1]
        whole[lo:hi, e, y, z] = total
        copies = []
        for step in range(1, n_line):
            copy = pltpu.make_async_remote_copy(
                src_ref=whole.at[lo:hi, e, y, z], dst_ref=whole.at[lo:hi, e, y, z],
                send_sem=gat_send.at[g, step - 1], recv_sem=gat_recv.at[g, step - 1],
                device_id=line(step), device_id_type=MESH)
            copy.start()
            copies.append(copy)
        gat_copies.append(copies)

    back_copies, core_copies, outs = [], {}, []

    def write_out(c, step):
        source = lax.rem(e + n_core - step, n_core)
        out = pltpu.make_async_copy(whole.at[c, source], gathered.at[c, source], out_sem.at[c, step])
        out.start()
        outs.append(out)

    def to_cores(g, side, half):
        lo, hi = GROUPS[g]
        for step in range(1, n_core):
            copy = pltpu.make_async_remote_copy(
                src_ref=whole.at[lo:hi, e, half], dst_ref=whole.at[lo:hi, e, half],
                send_sem=core_send.at[g, side, step - 1], recv_sem=core_recv.at[g, side, step - 1],
                device_id={"examples": lax.rem(e + step, n_core)}, device_id_type=MESH)
            copy.start()
            core_copies[(g, side, step)] = copy

    for g, (lo, hi) in enumerate(GROUPS):
        for copy in gat_copies[g]:
            copy.wait_recv()
        copy = pltpu.make_async_remote_copy(
            src_ref=whole.at[lo:hi, e, y], dst_ref=whole.at[lo:hi, e, y], send_sem=back_send.at[g],
            recv_sem=back_recv.at[g], device_id=pair, device_id_type=MESH)
        copy.start()
        back_copies.append(copy)
        to_cores(g, 0, y)
    for g, (lo, hi) in enumerate(GROUPS):
        back_copies[g].wait_recv()
        to_cores(g, 1, 1 - y)
        for c in range(lo, hi):
            write_out(c, 0)
    for g, (lo, hi) in enumerate(GROUPS):
        for side in range(2):
            for step in range(1, n_core):
                core_copies[(g, side, step)].wait_recv()
        for c in range(lo, hi):
            for step in range(1, n_core):
                write_out(c, step)
    for out in outs:
        out.wait()
    for copies in [pair_copies, back_copies, list(core_copies.values())] + line_copies + gat_copies:
        for copy in copies:
            copy.wait_send()


def split_lanes(value):
    high = value.astype(jnp.bfloat16)
    low = (value - high.astype(jnp.float32)).astype(jnp.bfloat16)
    return high, low


def features_of(grad_pair, act_tile, first, columns, seq_len, width_in):
    width_out = grad_pair.shape[1] // 2
    batch = grad_pair.shape[0] // seq_len
    tile = min(TILE, columns)
    pieces = []
    offset = lax.broadcasted_iota(jnp.int32, (width_out, tile), 0) - lax.broadcasted_iota(
        jnp.int32, (width_out, tile), 1) // width_in
    for start in range(0, columns, tile):
        pick = jnp.where(offset == first + start // width_in, 1.0, 0.0).astype(jnp.bfloat16)
        pick = jnp.concatenate([pick, pick], axis=0)
        spread = jnp.dot(grad_pair[...], pick, preferred_element_type=jnp.float32)
        for part in range(0, tile, LANES):
            piece = spread[:, part:part + LANES] * act_tile[...]
            pieces.append(piece.reshape(seq_len, batch, LANES).sum(axis=0))
    return jnp.concatenate(pieces, axis=1)


def gram_kernel(n_tensor, n_core, seq_len, width_in, block, slots,
                gathered, feat_up, gram_up, feat_down, gram_down,
                rows, grad_pair, act_tile, own_grad, own_act, right, left_even, left_odd, own_feat, held, load_sem, feat_sem, gram_sem):
    t = lax.axis_index("tensor")
    e = lax.axis_index("examples")
    n_line = n_tensor // 2
    batch = gathered.shape[1] // seq_len
    width_out = gathered.shape[2]
    own = own_grad.shape[0] // seq_len
    total_examples = batch
    a_rows = width_out // n_core
    a_cols = width_out // n_tensor
    a_block = block // width_in
    n_blocks = a_rows // a_block
    feat_part = own_feat.shape[2] // n_blocks
    a_part = feat_part // width_in
    own_at = pl.multiple_of((e * n_tensor + (t % 2) * n_line + t // 2) * (own * seq_len), own * seq_len)
    scale = 1.0 / math.sqrt(seq_len)

    loads = [pltpu.make_async_copy(gathered.at[c], rows.at[c], load_sem.at[c]) for c in range(3)]
    for c in (2, 1, 0):
        loads[c].start()
    loads[2].wait()

    for layer, (gram, feat) in enumerate(((gram_up, feat_up), (gram_down, feat_down))):
        chunk = 1 - layer
        loads[chunk].wait()
        lane = lax.broadcasted_iota(jnp.int32, (batch, LANES), 1)
        for s in range(seq_len):
            at = pl.ds(s * batch, batch)
            high, low = split_lanes(rows[chunk, pl.ds(s, batch, seq_len), :])
            grad_pair[at, :width_out] = high
            grad_pair[at, width_out:] = low
            act = rows[2, pl.ds(s, batch, seq_len), :] * scale
            turned = pltpu.roll(act, width_in, axis=1)
            first, second = (act, turned) if layer == 0 else (turned, act)
            act_tile[at, :] = jnp.where(lane < width_in, first, second)
        lane = lax.broadcasted_iota(jnp.int32, (own, LANES), 1)
        grads, acts = [], []
        for s in range(seq_len):
            grads.append(rows[chunk, pl.ds(own_at + s, own, seq_len), :])
            act = rows[2, pl.ds(own_at + s, own, seq_len), :] * scale
            turned = pltpu.roll(act, width_in, axis=1)
            first, second = (act, turned) if layer == 0 else (turned, act)
            acts.append(jnp.where(lane < width_in, first, second))
        high, low = split_lanes(jnp.concatenate(grads, axis=0))
        own_grad[:, :width_out] = high
        own_grad[:, width_out:] = low
        own_act[...] = jnp.concatenate(acts, axis=0)

        columns = a_cols * width_in
        value = features_of(grad_pair, act_tile, t * a_cols, columns, seq_len, width_in)
        high, low = split_lanes(value * (1.0 / total_examples))
        right[0:batch] = high
        right[batch:2 * batch] = low
        right[2 * batch:3 * batch] = high
        if right.shape[0] > 3 * batch:
            right[3 * batch:] = jnp.zeros((right.shape[0] - 3 * batch, columns), jnp.bfloat16)

        def prepare(i, target):
            value = features_of(grad_pair, act_tile, e * a_rows + i * a_block, block, seq_len, width_in)
            high, low = split_lanes(value)
            high, low = high.astype(jnp.float32), low.astype(jnp.float32)
            left = [high, high, low]
            if right.shape[0] > 3 * batch:
                left.append(jnp.zeros((right.shape[0] - 3 * batch, block), jnp.float32))
            target[...] = jnp.concatenate(left, axis=0).T.astype(jnp.bfloat16)

        def step(i, current, following):
            slot = lax.rem(i + layer * n_blocks, slots)

            def wait():
                pltpu.make_async_copy(held.at[slot], gram.at[pl.ds(0, block)], gram_sem.at[slot]).wait()

            if layer == 0:
                pl.when(i >= slots)(wait)
            else:
                wait()
            for start in range(0, columns, TILE):
                held[slot, :, start:start + TILE] = jnp.dot(
                    current[...], right[:, start:start + TILE], preferred_element_type=jnp.float32)
            prepare(lax.rem(i + 1, n_blocks), following)
            value = features_of(own_grad, own_act, i * a_part, feat_part, seq_len, width_in)
            own_feat[layer, :, pl.ds(pl.multiple_of(i * feat_part, feat_part), feat_part)] = value
            pltpu.make_async_copy(
                held.at[slot], gram.at[pl.ds(pl.multiple_of(i * block, block), block)], gram_sem.at[slot]).start()

        def two_steps(i, carry):
            step(2 * i, left_even, left_odd)
            step(2 * i + 1, left_odd, left_even)
            return carry

        prepare(0, left_even)
        lax.fori_loop(0, n_blocks // 2, two_steps, 0)
        pltpu.make_async_copy(own_feat.at[layer], feat, feat_sem.at[layer]).start()

    for slot in range(slots):
        pltpu.make_async_copy(held.at[slot], gram_down.at[pl.ds(0, block)], gram_sem.at[slot]).wait()
    for layer, feat in enumerate((feat_up, feat_down)):
        pltpu.make_async_copy(own_feat.at[layer], feat, feat_sem.at[layer]).wait()


def shards(n_tensor, n_core, act_up, grad_up, act_down, grad_down, b_au, b_gu, b_ad, b_gd):
    ex_local, seq_len = act_up.shape[0], act_up.shape[1]
    token_rows = ex_local * seq_len
    acts = [a.reshape(token_rows, a.shape[2]) for a in (act_up, grad_up, act_down, grad_down)]
    bases = [b_au.T, b_gu, b_ad.T, b_gd]
    width_in, width_out = b_au.shape[1], b_gu.shape[1]
    own_rows = token_rows // n_tensor
    owned = own_rows // seq_len
    n_line = n_tensor // 2
    f32 = jnp.float32
    any_space = pl.BlockSpec(memory_space=pl.ANY)
    dma = pltpu.SemaphoreType.DMA
    steps = max(n_line - 1, 1)
    gathered = pl.pallas_call(
        functools.partial(exchange_kernel, n_tensor, n_core, own_rows),
        out_shape=jax.ShapeDtypeStruct((3, n_core, 2, n_line, own_rows, LANES), f32),
        in_specs=[any_space] * 8,
        out_specs=any_space,
        scratch_shapes=[pltpu.VMEM(a.shape, a.dtype) for a in acts + bases] + [
            pltpu.VMEM((3, 2, n_line, own_rows, LANES), f32),
            pltpu.VMEM((3, n_line, own_rows, LANES), f32),
            pltpu.VMEM((3, steps, own_rows, LANES), f32),
            pltpu.VMEM((3, n_core, 2, n_line, own_rows, LANES), f32),
            dma((8,)), dma((3, n_core)),
            dma((3,)), dma((3,)), dma((3, steps)), dma((3, steps)), dma((3, steps)), dma((3, steps)),
            dma((3,)), dma((3,)), dma((3, 2, n_core - 1)), dma((3, 2, n_core - 1)),
        ],
        compiler_params=pltpu.CompilerParams(
            collective_id=0, has_side_effects=True, vmem_limit_bytes=VMEM_LIMIT),
        name="project_and_gather",
    )(*acts, *bases)

    tokens = n_core * token_rows
    batch = tokens // seq_len
    feat = width_in * width_out
    row_width, col_width = feat // n_core, feat // n_tensor
    block, slots = 512, 4
    depth = -(-3 * batch // LANES) * LANES
    shape = jax.ShapeDtypeStruct
    bf16 = jnp.bfloat16
    feature_one, gram_one, feature_two, gram_two = pl.pallas_call(
        functools.partial(gram_kernel, n_tensor, n_core, seq_len, width_in, block, slots),
        out_shape=[shape((owned, feat), f32), shape((row_width, col_width), f32)] * 2,
        in_specs=[any_space],
        out_specs=[any_space] * 4,
        scratch_shapes=[
            pltpu.VMEM((3, tokens, LANES), f32),
            pltpu.VMEM((tokens, 2 * width_out), bf16),
            pltpu.VMEM((tokens, LANES), f32),
            pltpu.VMEM((own_rows, 2 * width_out), bf16),
            pltpu.VMEM((own_rows, LANES), f32),
            pltpu.VMEM((depth, col_width), bf16),
            pltpu.VMEM((block, depth), bf16),
            pltpu.VMEM((block, depth), bf16),
            pltpu.VMEM((2, owned, feat), f32),
            pltpu.VMEM((slots, block, col_width), f32),
            dma((3,)), dma((2,)), dma((slots,)),
        ],
        compiler_params=pltpu.CompilerParams(vmem_limit_bytes=VMEM_LIMIT),
        name="features_and_gram",
    )(gathered.reshape(3, tokens, LANES))
    return (
        feature_one.reshape(1, owned, feat),
        gram_one,
        feature_two.reshape(1, owned, feat),
        gram_two,
    )


def solution(mesh):
    in_specs = (
        P(("groups", "examples"), None, "tensor"),
        P(("groups", "examples"), None, "tensor"),
        P(("groups", "examples"), None, "tensor"),
        P(("groups", "examples"), None, "tensor"),
        P("tensor", None),
        P("tensor", None),
        P("tensor", None),
        P("tensor", None),
    )
    out_specs = (
        P(("groups", "examples"), "tensor", None),
        P(("groups", "examples"), "tensor"),
        P(("groups", "examples"), "tensor", None),
        P(("groups", "examples"), "tensor"),
    )
    body = functools.partial(shards, mesh.shape["tensor"], mesh.shape["examples"])
    return jax.shard_map(body, mesh=mesh, in_specs=in_specs, out_specs=out_specs, check_vma=False)
```
